32 devices in a mesh: vox: 8 (over z, x), rep: 4 (over y, core).
Axes of the slice: x: 2, y: 2, z: 4, core: 2. Of those that a mesh axis runs over, the one named last changes fastest.
Arguments:
- fine_feats: bfloat16 [4, 32768, 192], P('rep', 'vox'), may hold values from -6 to 6
- occupancy: int32 [4, 32768], P('rep', 'vox'), may hold values 0 or 1
- parent: int32 [4, 4096], P('rep', 'vox'), may hold values from 0 to 4095, as said below
- neighbors: int32 [4, 27, 4096], P('rep', None, 'vox'), may hold values from -1 to 4095, as said below
- cotangent: bfloat16 [4, 32768, 192], P('rep', 'vox'), may hold values from -0.046875 to 0.046875
- down_weight: bfloat16 [8, 192, 192], replicated, may hold values from -0.21875 to 0.21875
- conv_weight: bfloat16 [27, 192, 192], replicated, may hold values from -0.15625 to 0.15625
- up_weight: bfloat16 [192, 8, 192], replicated, may hold values from -0.4375 to 0.4375
Outputs:
- grad_down: bfloat16 [8, 192, 192], replicated
- grad_conv: bfloat16 [27, 192, 192], replicated
- grad_up: bfloat16 [192, 8, 192], replicated
The draws below stay inside these ranges and needn't reach their ends.
Inputs may be any that keep to these rules, and one draw needn't show every extreme that they name: Each scene's ids 0 to 4095 each appear exactly once; the parent of a group on vox index d is owned by index parent // 512; the groups of one device name at most 2 parents owned by any one other device, and in every draw some device names exactly 2 at some other device. `neighbors`: entry 13 is the coarse voxel itself; every present neighbor is owned by the same vox index or one of the two next to it.
All inputs are finite; a program needn't handle non-finite values. No bound on the sum of `occupancy` on one device may be relied on, other than what follows from the above.
Results may differ from the reference program's by a relative error of at most 0.0095.
Values may be sent and summed in bfloat16 or wider, within the bound.
A program may use at most 128 MiB of HBM per device.

```python
import jax
import jax.numpy as jnp

CH = 192
COARSE_DEV = 512
CAP = 2
FINE = 32768
COARSE = 4096
SCENES = 4
N_VOX = 8
N_REP = 4


def distinct_order(key, count_rows, count_cols):
    scores = jax.random.randint(key, (count_rows, count_cols), 0, 1 << 20)
    scores = scores * count_cols + jnp.arange(count_cols, dtype=jnp.int32)[None, :]
    return jnp.argsort(scores, axis=1).astype(jnp.int32)


def parent_scene(key):
    owners = N_VOX
    group_count = COARSE_DEV
    keys = jax.random.split(key, 5)
    upper_counts = jnp.triu(jax.random.randint(keys[0], (owners, owners), 0, CAP + 1), 1)
    counts = upper_counts + upper_counts.T
    first = jax.random.randint(keys[1], (), 0, owners)
    second = (first + 1 + jax.random.randint(keys[2], (), 0, owners - 1)) % owners
    counts = counts.at[first, second].set(CAP).at[second, first].set(CAP)
    out_total = jnp.sum(counts, axis=1)
    local_count = group_count - out_total
    start_in = local_count[None, :] + jnp.cumsum(counts, axis=0) - counts
    cum_out = jnp.cumsum(counts, axis=1)
    start_out = cum_out - counts
    slot_perm = distinct_order(keys[3], owners, group_count)
    row_index = jnp.arange(group_count, dtype=jnp.int32)

    def one_device(device, cum_row, start_out_row, start_in_row, total_row):
        dest = jnp.clip(jnp.searchsorted(cum_row, row_index, side='right').astype(jnp.int32), 0, owners - 1)
        offset = row_index - start_out_row[dest]
        slot_remote = jnp.clip(start_in_row[dest] + offset, 0, group_count - 1)
        remote_id = dest * group_count + slot_perm[dest, slot_remote]
        local_slot = jnp.clip(row_index - total_row, 0, group_count - 1)
        local_id = device * group_count + slot_perm[device, local_slot]
        return jnp.where(row_index < total_row, remote_id, local_id)
    devices = jnp.arange(owners, dtype=jnp.int32)
    ids = jax.vmap(one_device)(devices, cum_out, start_out, start_in, out_total)
    shuffle = distinct_order(keys[4], owners, group_count)
    ids = jnp.take_along_axis(ids, shuffle, axis=1)
    return ids.reshape(-1).astype(jnp.int32)


def draw_parent(key, part):
    scenes = [parent_scene(jax.random.fold_in(key, 101 + scene)) for scene in range(N_REP)]
    return jnp.stack(scenes)


def neighbor_scene(key):
    total = N_VOX * COARSE_DEV
    keys = jax.random.split(key, 3)
    present = jax.random.randint(keys[0], (27, total), 0, 3) == 0
    pick = jax.random.randint(keys[1], (27, total), 0, 4)
    step = jnp.where(pick == 0, -1, jnp.where(pick == 3, 1, 0))
    own_ids = jnp.arange(total, dtype=jnp.int32)
    owner = own_ids // COARSE_DEV
    moved = owner[None, :] + step
    moved = jnp.where((moved < 0) | (moved >= N_VOX), owner[None, :], moved)
    local_ids = jax.random.randint(keys[2], (27, total), 0, COARSE_DEV)
    ids = jnp.where(present, moved * COARSE_DEV + local_ids, -1)
    ids = ids.at[13].set(own_ids)
    return ids.astype(jnp.int32)


def draw_neighbors(key, part):
    scenes = [neighbor_scene(jax.random.fold_in(key, 202 + scene)) for scene in range(N_REP)]
    return jnp.stack(scenes)


def plant(array, rng, low, high):
    longest = array.shape.index(max(array.shape))
    spots = []
    for shift in (0, 1):
        where = [jax.random.randint(jax.random.fold_in(rng, axis), (), 0, length) for axis, length in enumerate(array.shape)]
        where[longest] = (where[longest] + shift) % array.shape[longest]
        spots.append(tuple(where))
    return array.at[spots[0]].set(low).at[spots[1]].set(high)


def levels(key, shape, cuts, smallest, high):
    def one(axis_at, blocks):
        draws = jax.random.uniform(jax.random.fold_in(jax.random.fold_in(key, 6), axis_at), (blocks,), jnp.float32, smallest / len(cuts), high / len(cuts))
        return jnp.repeat(jnp.exp(draws), shape[axis_at] // blocks).reshape((-1,) + (1,) * (len(shape) - axis_at - 1))

    level = one(*cuts[0])
    for cut in cuts[1:]:
        level = level * one(*cut)
    return level


def normal_values(key, dims, width, reach, cuts=(), kind=jnp.bfloat16):
    drawn = width * jax.random.normal(key, dims, jnp.float32)
    if cuts:
        drawn = drawn * levels(key, dims, cuts, -0.22, 0.18)
    return jnp.clip(drawn, -reach, reach).astype(kind)


def setup_inputs(seed: int = 0) -> dict:
    arg_keys = jax.random.split(jax.random.key(seed), 9)
    return {
        "fine_feats": normal_values(arg_keys[0], (SCENES, FINE, CH), 1.0, 6.0, ((0, 4), (1, 8))),
        "occupancy": plant((jax.random.randint(arg_keys[1], (SCENES, FINE), 0, 2) < 1).astype(jnp.int32), jax.random.fold_in(arg_keys[1], 1), 0, 1),
        "parent": draw_parent(jax.random.fold_in(arg_keys[8], 71), 0),
        "neighbors": draw_neighbors(jax.random.fold_in(arg_keys[8], 71), 0),
        "cotangent": normal_values(arg_keys[4], (SCENES, FINE, CH), (1.0 / (N_REP * COARSE) ** 0.5), 0.046875, ((0, 4), (1, 8))),
        "down_weight": normal_values(arg_keys[5], (8, CH, CH), (4 * CH) ** -0.5, 0.21875),
        "conv_weight": normal_values(arg_keys[6], (27, CH, CH), (9 * CH) ** -0.5, 0.15625),
        "up_weight": normal_values(arg_keys[7], (CH, 8, CH), CH ** -0.5, 0.4375),
    }


def silu_slope(values):
    sig = jax.nn.sigmoid(values)
    return sig * (1.0 + values * (1.0 - sig))


def scene_terms(fine_rows, occupied, parents, near_ids, cot_rows, down_weight, conv_weight, up_weight):
    channels = fine_rows.shape[-1]
    mask_half = occupied.astype(jnp.bfloat16)[:, None]
    grouped = (fine_rows * mask_half).reshape(COARSE, 8 * channels)
    pre_groups = jnp.dot(grouped, down_weight.reshape(8 * channels, channels), preferred_element_type=jnp.float32)
    pre = jnp.zeros((COARSE, channels), jnp.float32).at[parents].add(pre_groups)
    hidden = jax.nn.silu(pre).astype(jnp.bfloat16)
    table = jnp.concatenate([hidden, jnp.zeros((1, channels), jnp.bfloat16)], 0)
    lookup = jnp.where(near_ids < 0, COARSE, near_ids).astype(jnp.int32)
    conv = jnp.zeros((COARSE, channels), jnp.float32)
    for offset in range(27):
        conv = conv + jnp.dot(table[lookup[offset]], conv_weight[offset], preferred_element_type=jnp.float32)
    upper = (hidden.astype(jnp.float32) + conv).astype(jnp.bfloat16)
    up_rows = upper[parents]
    cot_groups = (cot_rows * mask_half).reshape(COARSE, 8 * channels)
    up_flat = up_weight.reshape(channels, 8 * channels)
    up_term = jnp.dot(up_rows.T, cot_groups, preferred_element_type=jnp.float32)
    back_groups = jnp.dot(cot_groups, up_flat.T, preferred_element_type=jnp.float32)
    grad_z = jnp.zeros((COARSE, channels), jnp.float32).at[parents].add(back_groups)
    dz_half = grad_z.astype(jnp.bfloat16)
    spread = jnp.zeros((COARSE + 1, channels), jnp.float32)
    conv_terms = []
    for offset in range(27):
        rows_here = table[lookup[offset]]
        conv_terms.append(jnp.dot(rows_here.T, dz_half, preferred_element_type=jnp.float32))
        spread = spread.at[lookup[offset]].add(jnp.dot(dz_half, conv_weight[offset].T, preferred_element_type=jnp.float32))
    grad_hidden = grad_z + spread[:COARSE]
    grad_pre = (grad_hidden * silu_slope(pre)).astype(jnp.bfloat16)
    down_term = jnp.dot(grouped.T, grad_pre[parents], preferred_element_type=jnp.float32)
    return down_term.reshape(8, channels, channels), jnp.stack(conv_terms), up_term.reshape(channels, 8, channels)


def reference(fine_feats, occupancy, parent, neighbors, cotangent, down_weight, conv_weight, up_weight):
    total_down = None
    for scene in range(SCENES):
        terms = scene_terms(fine_feats[scene], occupancy[scene], parent[scene], neighbors[scene], cotangent[scene], down_weight, conv_weight, up_weight)
        if total_down is None:
            total_down, total_conv, total_up = terms
        else:
            total_down = total_down + terms[0]
            total_conv = total_conv + terms[1]
            total_up = total_up + terms[2]
    return (total_down.astype(jnp.bfloat16), total_conv.astype(jnp.bfloat16), total_up.astype(jnp.bfloat16))
```

```python
import jax
import jax.numpy as jnp
from jax import lax
from jax.experimental import pallas as pl
from jax.experimental.pallas import tpu as pltpu
from jax.sharding import PartitionSpec as P

CAP = 2


def dot(left, right, dims, precision=None):
    return lax.dot_general(
        left, right, (dims, ((), ())), precision=precision, preferred_element_type=jnp.float32
    )


def conv_kernel(
    before, own, after, wide, ids_out, ids_in, weight, term_ref, both_ref, acc_up, acc_down
):
    step = pl.program_id(0)
    channels, count = acc_up.shape

    @pl.when(step == 0)
    def _():
        acc_up[...] = jnp.zeros_like(acc_up)
        acc_down[...] = jnp.zeros_like(acc_down)

    rows = lax.broadcasted_iota(jnp.int32, (count, count), 0)

    def hot(ids):
        return jnp.where(rows == ids, 1.0, 0.0).astype(jnp.bfloat16)

    weight_here = weight[0]
    gathered = jnp.zeros((channels, count), jnp.float32)
    spread = acc_down[...]
    for at, block in enumerate((before, own, after)):
        gathered += dot(
            block[:channels, :], hot(ids_out[0] - at * count), ((1,), (0,))
        )
        moved = dot(weight_here, block[channels:, :], ((1,), (0,))).astype(jnp.bfloat16)
        spread += dot(moved, hot(ids_in[0, :, at * count : (at + 1) * count]), ((1,), (1,)))
    acc_down[...] = spread
    gathered = gathered.astype(jnp.bfloat16)
    acc_up[...] += dot(weight_here, gathered, ((0,), (0,)))
    term_ref[0] = dot(gathered, own[channels:, :], ((1,), (1,)))

    @pl.when(step == pl.num_programs(0) - 1)
    def _():
        upper = own[:channels, :].astype(jnp.float32) + acc_up[...]
        both_ref[:channels, :] = upper.astype(jnp.bfloat16)
        pre = wide[:channels, :]
        sig = jax.nn.sigmoid(pre)
        slope = sig * (1.0 + pre * (1.0 - sig))
        both_ref[channels:, :] = ((wide[channels:, :] + acc_down[...]) * slope).astype(
            jnp.bfloat16
        )


def conv_call(before, own, after, wide, ids_out, ids_in, conv_weight):
    offsets, channels = conv_weight.shape[:2]
    count = own.shape[1]
    whole = lambda j: (0, 0)
    each = lambda j: (j, 0, 0)
    return pl.pallas_call(
        conv_kernel,
        grid=(offsets,),
        in_specs=[pl.BlockSpec((2 * channels, count), whole)] * 4
        + [
            pl.BlockSpec((1, 1, count), each),
            pl.BlockSpec((1, 1, 3 * count), each),
            pl.BlockSpec((1, channels, channels), each),
        ],
        out_specs=[
            pl.BlockSpec((1, channels, channels), each),
            pl.BlockSpec((2 * channels, count), whole),
        ],
        out_shape=[
            jax.ShapeDtypeStruct((offsets, channels, channels), jnp.float32),
            jax.ShapeDtypeStruct((2 * channels, count), jnp.bfloat16),
        ],
        scratch_shapes=[pltpu.VMEM((channels, count), jnp.float32)] * 2,
        compiler_params=pltpu.CompilerParams(vmem_limit_bytes=48 * 1024 * 1024),
    )(before, own, after, wide, ids_out, ids_in, conv_weight)


def per_device(
    fine_feats, occupancy, parent, neighbors, cotangent, down_weight, conv_weight, up_weight
):
    fine_rows = fine_feats[0]
    occupied = occupancy[0]
    parents = parent[0]
    near_ids = neighbors[0]
    cot_rows = cotangent[0]
    channels = fine_rows.shape[1]
    count = parents.shape[0]
    vox_count = lax.axis_size("vox")
    slots = vox_count * CAP
    own_index = lax.axis_index("vox")
    up = [(i, i + 1) for i in range(vox_count - 1)]
    down = [(j, i) for i, j in up]
    exact = lax.Precision.HIGHEST

    near_next = near_ids + 1
    lists = jnp.concatenate(
        [lax.ppermute(near_next, "vox", up), near_next, lax.ppermute(near_next, "vox", down)], 1
    )
    ids_in = (lists - 1 - own_index * count)[:, None, :]
    ids_out = jnp.where(near_ids < 0, -1, near_ids - (own_index - 1) * count)[:, None, :]

    owner = parents // count
    local_id = parents % count
    remote = owner != own_index
    owner_hits = (
        (owner[:, None] == jnp.arange(vox_count, dtype=jnp.int32)[None, :]) & remote[:, None]
    ).astype(jnp.int32)
    ranks = jnp.cumsum(owner_hits, axis=0) - 1
    slot = jnp.sum(ranks * owner_hits, axis=1)
    dest = jnp.where(remote, owner * CAP + slot, slots)
    place = jnp.arange(slots, dtype=jnp.int32)[:, None] == dest[None, :]
    send_ids = jnp.sum(jnp.where(place, local_id[None, :] + 1, 0), axis=1)

    mask_half = occupied.astype(jnp.bfloat16)[:, None]
    grouped = (fine_rows * mask_half).reshape(count, 8 * channels)
    cot_groups = (cot_rows * mask_half).reshape(count, 8 * channels)
    pre_groups = dot(grouped, down_weight.reshape(8 * channels, channels), ((1,), (0,)))
    back_groups = dot(cot_groups, up_weight.reshape(channels, 8 * channels), ((1,), (1,)))
    values = jnp.concatenate([pre_groups, back_groups], 1)
    send = dot(place.astype(jnp.float32), values, ((1,), (0,)), exact)
    tail = jnp.broadcast_to(send_ids.astype(jnp.float32)[:, None], (slots, 128))
    send = jnp.concatenate([send, tail], 1).reshape(vox_count, CAP, 2 * channels + 128)
    got = lax.all_to_all(send, "vox", split_axis=0, concat_axis=0, tiled=True)
    got = got.reshape(slots, 2 * channels + 128)
    recv_index = got[:, 2 * channels].astype(jnp.int32) - 1
    coarse_ids = jnp.arange(count, dtype=jnp.int32)[:, None]
    keep = coarse_ids == jnp.where(remote, -1, local_id)[None, :]
    arrived = coarse_ids == recv_index[None, :]
    wide = dot(values, keep.astype(jnp.float32), ((0,), (1,)), exact) + dot(
        got[:, : 2 * channels], arrived.astype(jnp.float32), ((0,), (1,)), exact
    )
    own = jnp.concatenate([jax.nn.silu(wide[:channels]), wide[channels:]], 0).astype(jnp.bfloat16)
    before = lax.ppermute(own, "vox", up)
    after = lax.ppermute(own, "vox", down)
    conv_term, both = conv_call(before, own, after, wide, ids_out, ids_in, conv_weight)

    outgoing = dot(arrived.astype(jnp.bfloat16), both, ((0,), (1,))).astype(jnp.bfloat16)
    returned = lax.all_to_all(
        outgoing.reshape(vox_count, CAP, 2 * channels),
        "vox",
        split_axis=0,
        concat_axis=0,
        tiled=True,
    ).reshape(slots, 2 * channels)
    rows = dot(both, keep.astype(jnp.bfloat16), ((1,), (0,))) + dot(
        returned, place.astype(jnp.bfloat16), ((0,), (0,))
    )
    rows = rows.astype(jnp.bfloat16)
    up_term = dot(rows[:channels], cot_groups, ((1,), (0,)))
    down_term = dot(grouped, rows[channels:], ((0,), (1,)))
    total_down, total_conv, total_up = lax.psum((down_term, conv_term, up_term), ("vox", "rep"))
    return (
        total_down.astype(jnp.bfloat16).reshape(8, channels, channels),
        total_conv.astype(jnp.bfloat16),
        total_up.astype(jnp.bfloat16).reshape(channels, 8, channels),
    )


def solution(mesh):
    return jax.shard_map(
        per_device,
        mesh=mesh,
        in_specs=(
            P("rep", "vox", None),
            P("rep", "vox"),
            P("rep", "vox"),
            P("rep", None, "vox"),
            P("rep", "vox", None),
            P(),
            P(),
            P(),
        ),
        out_specs=(P(), P(), P()),
        check_vma=False,
    )
```

```python
import jax
import jax.numpy as jnp
from jax import lax
from jax.experimental import pallas as pl
from jax.experimental.pallas import tpu as pltpu
from jax.sharding import PartitionSpec as P

CAP = 2


def dot(left, right, dims, precision=None):
    return lax.dot_general(
        left, right, (dims, ((), ())), precision=precision, preferred_element_type=jnp.float32
    )


def conv_kernel(
    before, own, after, wide, ids_out, ids_in, weight, term_ref, both_ref, acc_up, acc_down
):
    step = pl.program_id(0)
    channels, count = acc_up.shape

    @pl.when(step == 0)
    def _():
        acc_up[...] = jnp.zeros_like(acc_up)
        acc_down[...] = jnp.zeros_like(acc_down)

    rows = lax.broadcasted_iota(jnp.int32, (count, count), 0)

    def hot(ids):
        return jnp.where(rows == ids, 1.0, 0.0).astype(jnp.bfloat16)

    weight_here = weight[0]
    gathered = jnp.zeros((channels, count), jnp.float32)
    spread = acc_down[...]
    for at, block in enumerate((before, own, after)):
        gathered += dot(
            block[:channels, :], hot(ids_out[0] - at * count), ((1,), (0,))
        )
        moved = dot(weight_here, block[channels:, :], ((1,), (0,))).astype(jnp.bfloat16)
        spread += dot(moved, hot(ids_in[0, :, at * count : (at + 1) * count]), ((1,), (1,)))
    acc_down[...] = spread
    gathered = gathered.astype(jnp.bfloat16)
    acc_up[...] += dot(weight_here, gathered, ((0,), (0,)))
    term_ref[0] = dot(gathered, own[channels:, :], ((1,), (1,)))

    @pl.when(step == pl.num_programs(0) - 1)
    def _():
        upper = own[:channels, :].astype(jnp.float32) + acc_up[...]
        both_ref[:channels, :] = upper.astype(jnp.bfloat16)
        pre = wide[:channels, :]
        sig = jax.nn.sigmoid(pre)
        slope = sig * (1.0 + pre * (1.0 - sig))
        both_ref[channels:, :] = ((wide[channels:, :] + acc_down[...]) * slope).astype(
            jnp.bfloat16
        )


def conv_call(before, own, after, wide, ids_out, ids_in, conv_weight):
    offsets, channels = conv_weight.shape[:2]
    count = own.shape[1]
    whole = lambda j: (0, 0)
    each = lambda j: (j, 0, 0)
    return pl.pallas_call(
        conv_kernel,
        grid=(offsets,),
        in_specs=[pl.BlockSpec((2 * channels, count), whole)] * 4
        + [
            pl.BlockSpec((1, 1, count), each),
            pl.BlockSpec((1, 1, 3 * count), each),
            pl.BlockSpec((1, channels, channels), each),
        ],
        out_specs=[
            pl.BlockSpec((1, channels, channels), each),
            pl.BlockSpec((2 * channels, count), whole),
        ],
        out_shape=[
            jax.ShapeDtypeStruct((offsets, channels, channels), jnp.float32),
            jax.ShapeDtypeStruct((2 * channels, count), jnp.bfloat16),
        ],
        scratch_shapes=[pltpu.VMEM((channels, count), jnp.float32)] * 2,
        compiler_params=pltpu.CompilerParams(vmem_limit_bytes=48 * 1024 * 1024),
    )(before, own, after, wide, ids_out, ids_in, conv_weight)


UNIT = 16
PIECES = (5 * UNIT, 4 * UNIT)
FAR = 4


def reduce_kernel(x_ref, out_ref, acc, got_core, got_one, got_two, got_far, send, recv):
    v, r = lax.axis_index("vox"), lax.axis_index("rep")
    z, x = v // 2, v % 2
    y, core = r // 2, r % 2
    core_peer = (v, y * 2 + (1 - core))
    y_peer = (v, (1 - y) * 2 + core)
    x_peer = (z * 2 + (1 - x), r)
    far_peers = [(((z + k) % FAR) * 2 + x, r) for k in range(1, FAR)]
    mesh_ids = pl.DeviceIdType.MESH

    barrier = pltpu.get_barrier_semaphore()
    peers = [core_peer, y_peer, x_peer] + far_peers
    for peer in peers:
        pl.semaphore_signal(barrier, inc=1, device_id=peer, device_id_type=mesh_ids)
    pl.semaphore_wait(barrier, len(peers))

    used = [0]

    def push(source, target, peer):
        at = used[0]
        used[0] += 1
        copy = pltpu.make_async_remote_copy(
            src_ref=source,
            dst_ref=target,
            send_sem=send.at[at],
            recv_sem=recv.at[at],
            device_id=peer,
            device_id_type=mesh_ids,
        )
        copy.start()
        return copy

    def at(start, size):
        return pl.ds(pl.multiple_of(start, UNIT), size)

    def add(target, target_at, left, left_at, others, size):
        def body(i, carry):
            step = i * UNIT
            total = left[at(left_at + step, UNIT), :].astype(jnp.float32)
            for ref, ref_at in others:
                total += ref[at(ref_at + step, UNIT), :].astype(jnp.float32)
            target[at(target_at + step, UNIT), :] = total.astype(target.dtype)
            return carry

        lax.fori_loop(0, size // UNIT, body, 0)

    half = 4 * FAR * sum(PIECES)
    base = [0, 4 * FAR * PIECES[0]]
    whole = [4 * FAR * p for p in PIECES]
    first_peer, second_peer = (y_peer, x_peer), (x_peer, y_peer)
    first_bit, second_bit = (y, x), (x, y)
    mine, other = core * half, (1 - core) * half
    sent = []

    core_copies = [
        push(x_ref.at[at(other + base[s], whole[s])], got_core.at[at(base[s], whole[s])], core_peer)
        for s in (0, 1)
    ]
    ones = []
    for s in (0, 1):
        core_copies[s].wait_recv()
        size = whole[s] // 2
        away = base[s] + (1 - first_bit[s]) * size
        add(acc, away, x_ref, mine + away, [(got_core, away)], size)
        ones.append(
            push(
                acc.at[at(away, size)],
                got_one.at[at(base[s] // 2, size)],
                first_peer[s],
            )
        )
        stay = base[s] + first_bit[s] * size
        add(acc, stay, x_ref, mine + stay, [(got_core, stay)], size)
    twos = []
    for s in (0, 1):
        ones[s].wait_recv()
        size = whole[s] // 4
        start = base[s] + first_bit[s] * (whole[s] // 2)
        away = (1 - second_bit[s]) * size
        add(acc, start + away, acc, start + away, [(got_one, base[s] // 2 + away)], size)
        twos.append(
            push(
                acc.at[at(start + away, size)],
                got_two.at[at(base[s] // 4, size)],
                second_peer[s],
            )
        )
        stay = second_bit[s] * size
        add(acc, start + stay, acc, start + stay, [(got_one, base[s] // 2 + stay)], size)
    fars = []
    for s in (0, 1):
        twos[s].wait_recv()
        size = whole[s] // 4
        start = base[s] + first_bit[s] * (whole[s] // 2) + second_bit[s] * size
        add(acc, start, acc, start, [(got_two, base[s] // 4)], size)
        copies = []
        for k in range(1, FAR):
            theirs = (z + k) % FAR
            copies.append(
                push(
                    acc.at[at(start + theirs * PIECES[s], PIECES[s])],
                    got_far.at[at((k - 1) * sum(PIECES) + s * PIECES[0], PIECES[s])],
                    far_peers[k - 1],
                )
            )
        fars.append(copies)
    back = []
    for s in (0, 1):
        for copy in fars[s]:
            copy.wait_recv()
        start = base[s] + first_bit[s] * (whole[s] // 2) + second_bit[s] * (whole[s] // 4)
        piece = start + z * PIECES[s]
        add(
            out_ref,
            mine + piece,
            acc,
            piece,
            [(got_far, k * sum(PIECES) + s * PIECES[0]) for k in range(FAR - 1)],
            PIECES[s],
        )
        span = at(mine + piece, PIECES[s])
        back.append([push(out_ref.at[span], out_ref.at[span], peer) for peer in far_peers])
    two_back = []
    for s in (0, 1):
        for copy in back[s]:
            copy.wait_recv()
        size = whole[s] // 4
        start = base[s] + first_bit[s] * (whole[s] // 2) + second_bit[s] * size
        span = at(mine + start, size)
        two_back.append(push(out_ref.at[span], out_ref.at[span], second_peer[s]))
    one_back = []
    for s in (0, 1):
        two_back[s].wait_recv()
        size = whole[s] // 2
        span = at(mine + base[s] + first_bit[s] * size, size)
        one_back.append(push(out_ref.at[span], out_ref.at[span], first_peer[s]))
    core_back = []
    for s in (0, 1):
        one_back[s].wait_recv()
        span = at(mine + base[s], whole[s])
        core_back.append(push(out_ref.at[span], out_ref.at[span], core_peer))
    for copy in core_back:
        copy.wait_recv()
    for copy in core_copies + ones + twos + fars[0] + fars[1]:
        copy.wait_send()
    for copy in back[0] + back[1] + two_back + one_back + core_back:
        copy.wait_send()


def reduce_call(partial):
    rows, columns = partial.shape
    assert rows == 8 * FAR * sum(PIECES)
    copies = 6 + 2 * (FAR - 1) + 6 + 2 * (FAR - 1)
    kind = partial.dtype
    return pl.pallas_call(
        reduce_kernel,
        in_specs=[pl.BlockSpec(memory_space=pltpu.VMEM)],
        out_specs=pl.BlockSpec(memory_space=pltpu.VMEM),
        out_shape=jax.ShapeDtypeStruct(partial.shape, kind),
        scratch_shapes=[
            pltpu.VMEM((rows // 2, columns), kind),
            pltpu.VMEM((rows // 2, columns), kind),
            pltpu.VMEM((rows // 4, columns), kind),
            pltpu.VMEM((rows // 8, columns), kind),
            pltpu.VMEM(((FAR - 1) * sum(PIECES), columns), kind),
            pltpu.SemaphoreType.DMA((copies,)),
            pltpu.SemaphoreType.DMA((copies,)),
        ],
        compiler_params=pltpu.CompilerParams(
            collective_id=0, has_side_effects=True, vmem_limit_bytes=40 * 1024 * 1024
        ),
    )(partial)


def total_gradients(down_term, conv_term, up_term):
    kids, channels = down_term.shape[0] // down_term.shape[1], down_term.shape[1]
    offsets = conv_term.shape[0]
    axes = ("vox", "rep")
    if lax.axis_size("vox") != 2 * FAR or lax.axis_size("rep") != 4:
        sums = lax.psum((down_term, conv_term, up_term), axes)
        return [total.astype(jnp.bfloat16) for total in sums]
    half = jnp.bfloat16
    wide = 2 * channels
    pairs = kids // 2
    up_rows = pairs * channels
    row_sets = jnp.concatenate(
        [conv_term.reshape(-1, channels).astype(half), down_term.astype(half)], 0
    )
    left = -(-(offsets + kids) // 2) * channels
    total_rows = 8 * FAR * sum(PIECES)
    left_rows = jnp.pad(row_sets[:left], ((0, total_rows - up_rows - left), (0, 0)))
    right_rows = jnp.pad(
        row_sets[left:], ((0, total_rows - up_rows - (row_sets.shape[0] - left)), (0, 0))
    )
    lower = jnp.concatenate([left_rows, right_rows], 1)
    ups = [up_term[:, p * wide : (p + 1) * wide].astype(half) for p in range(pairs)]
    done = reduce_call(jnp.concatenate(ups + [lower], 0))
    up_total = jnp.concatenate(
        [done[p * channels : (p + 1) * channels] for p in range(pairs)], 1
    )
    rest = done[up_rows : up_rows + left]
    conv_right = offsets * channels - left
    conv_total = jnp.concatenate([rest[:, :channels], rest[:conv_right, channels:]], 0)
    down_total = rest[conv_right : conv_right + kids * channels, channels:]
    return down_total, conv_total.reshape(offsets, channels, channels), up_total


def per_device(
    fine_feats, occupancy, parent, neighbors, cotangent, down_weight, conv_weight, up_weight
):
    fine_rows = fine_feats[0]
    occupied = occupancy[0]
    parents = parent[0]
    near_ids = neighbors[0]
    cot_rows = cotangent[0]
    channels = fine_rows.shape[1]
    count = parents.shape[0]
    vox_count = lax.axis_size("vox")
    slots = vox_count * CAP
    own_index = lax.axis_index("vox")
    up = [(i, i + 1) for i in range(vox_count - 1)]
    down = [(j, i) for i, j in up]
    exact = lax.Precision.HIGHEST

    near_next = near_ids + 1
    lists = jnp.concatenate(
        [lax.ppermute(near_next, "vox", up), near_next, lax.ppermute(near_next, "vox", down)], 1
    )
    ids_in = (lists - 1 - own_index * count)[:, None, :]
    ids_out = jnp.where(near_ids < 0, -1, near_ids - (own_index - 1) * count)[:, None, :]

    owner = parents // count
    local_id = parents % count
    remote = owner != own_index
    owner_hits = (
        (owner[:, None] == jnp.arange(vox_count, dtype=jnp.int32)[None, :]) & remote[:, None]
    ).astype(jnp.int32)
    ranks = jnp.cumsum(owner_hits, axis=0) - 1
    slot = jnp.sum(ranks * owner_hits, axis=1)
    dest = jnp.where(remote, owner * CAP + slot, slots)
    place = jnp.arange(slots, dtype=jnp.int32)[:, None] == dest[None, :]
    send_ids = jnp.sum(jnp.where(place, local_id[None, :] + 1, 0), axis=1)

    mask_half = occupied.astype(jnp.bfloat16)[:, None]
    grouped = (fine_rows * mask_half).reshape(count, 8 * channels)
    cot_groups = (cot_rows * mask_half).reshape(count, 8 * channels)
    pre_groups = dot(grouped, down_weight.reshape(8 * channels, channels), ((1,), (0,)))
    back_groups = dot(cot_groups, up_weight.reshape(channels, 8 * channels), ((1,), (1,)))
    values = jnp.concatenate([pre_groups, back_groups], 1)
    send = dot(place.astype(jnp.float32), values, ((1,), (0,)), exact)
    tail = jnp.broadcast_to(send_ids.astype(jnp.float32)[:, None], (slots, 128))
    send = jnp.concatenate([send, tail], 1).reshape(vox_count, CAP, 2 * channels + 128)
    got = lax.all_to_all(send, "vox", split_axis=0, concat_axis=0, tiled=True)
    got = got.reshape(slots, 2 * channels + 128)
    recv_index = got[:, 2 * channels].astype(jnp.int32) - 1
    coarse_ids = jnp.arange(count, dtype=jnp.int32)[:, None]
    keep = coarse_ids == jnp.where(remote, -1, local_id)[None, :]
    arrived = coarse_ids == recv_index[None, :]
    wide = dot(values, keep.astype(jnp.float32), ((0,), (1,)), exact) + dot(
        got[:, : 2 * channels], arrived.astype(jnp.float32), ((0,), (1,)), exact
    )
    own = jnp.concatenate([jax.nn.silu(wide[:channels]), wide[channels:]], 0).astype(jnp.bfloat16)
    before = lax.ppermute(own, "vox", up)
    after = lax.ppermute(own, "vox", down)
    conv_term, both = conv_call(before, own, after, wide, ids_out, ids_in, conv_weight)

    outgoing = dot(arrived.astype(jnp.bfloat16), both, ((0,), (1,))).astype(jnp.bfloat16)
    returned = lax.all_to_all(
        outgoing.reshape(vox_count, CAP, 2 * channels),
        "vox",
        split_axis=0,
        concat_axis=0,
        tiled=True,
    ).reshape(slots, 2 * channels)
    rows = dot(both, keep.astype(jnp.bfloat16), ((1,), (0,))) + dot(
        returned, place.astype(jnp.bfloat16), ((0,), (0,))
    )
    rows = rows.astype(jnp.bfloat16)
    up_term = dot(rows[:channels], cot_groups, ((1,), (0,)))
    down_term = dot(grouped, rows[channels:], ((0,), (1,)))
    total_down, total_conv, total_up = total_gradients(down_term, conv_term, up_term)
    return (
        total_down.reshape(8, channels, channels),
        total_conv,
        total_up.reshape(channels, 8, channels),
    )


def solution(mesh):
    return jax.shard_map(
        per_device,
        mesh=mesh,
        in_specs=(
            P("rep", "vox", None),
            P("rep", "vox"),
            P("rep", "vox"),
            P("rep", None, "vox"),
            P("rep", "vox", None),
            P(),
            P(),
            P(),
        ),
        out_specs=(P(), P(), P()),
        check_vma=False,
    )
```

```python
import functools

import jax
import jax.numpy as jnp
from jax import lax
from jax.experimental import pallas as pl
from jax.experimental.pallas import tpu as pltpu
from jax.sharding import PartitionSpec as P

CAP = 2


def dot(left, right, dims, precision=None):
    return lax.dot_general(
        left, right, (dims, ((), ())), precision=precision, preferred_element_type=jnp.float32
    )


def conv_kernel(
    before, own, after, wide, ids_out, ids_in, weight, term_ref, both_ref, acc_up, acc_down
):
    step = pl.program_id(0)
    channels, count = acc_up.shape

    @pl.when(step == 0)
    def _():
        acc_up[...] = jnp.zeros_like(acc_up)
        acc_down[...] = jnp.zeros_like(acc_down)

    rows = lax.broadcasted_iota(jnp.int32, (count, count), 0)

    def hot(ids):
        return jnp.where(rows == ids, 1.0, 0.0).astype(jnp.bfloat16)

    weight_here = weight[0]
    gathered = jnp.zeros((channels, count), jnp.float32)
    spread = acc_down[...]
    for at, block in enumerate((before, own, after)):
        gathered += dot(
            block[:channels, :], hot(ids_out[0] - at * count), ((1,), (0,))
        )
        moved = dot(weight_here, block[channels:, :], ((1,), (0,))).astype(jnp.bfloat16)
        spread += dot(moved, hot(ids_in[0, :, at * count : (at + 1) * count]), ((1,), (1,)))
    acc_down[...] = spread
    gathered = gathered.astype(jnp.bfloat16)
    acc_up[...] += dot(weight_here, gathered, ((0,), (0,)))
    term = dot(gathered, own[channels:, :], ((1,), (1,))).astype(term_ref.dtype)

    @pl.when(step % 2 == 0)
    def _():
        term_ref[:, :channels] = term
        term_ref[:, channels:] = jnp.zeros_like(term)

    @pl.when(step % 2 == 1)
    def _():
        term_ref[:, channels:] = term

    @pl.when(step == pl.num_programs(0) - 1)
    def _():
        upper = own[:channels, :].astype(jnp.float32) + acc_up[...]
        both_ref[:channels, :] = upper.astype(jnp.bfloat16)
        pre = wide[:channels, :]
        sig = jax.nn.sigmoid(pre)
        slope = sig * (1.0 + pre * (1.0 - sig))
        both_ref[channels:, :] = ((wide[channels:, :] + acc_down[...]) * slope).astype(
            jnp.bfloat16
        )


def conv_call(packed_rows, before, own, after, wide, ids_out, ids_in, conv_weight):
    offsets, channels = conv_weight.shape[:2]
    count = own.shape[1]
    whole = lambda j: (0, 0)
    each = lambda j: (j, 0, 0)
    return pl.pallas_call(
        conv_kernel,
        grid=(offsets,),
        in_specs=[pl.BlockSpec((2 * channels, count), whole)] * 4
        + [
            pl.BlockSpec((1, 1, count), each),
            pl.BlockSpec((1, 1, 3 * count), each),
            pl.BlockSpec((1, channels, channels), each),
        ],
        out_specs=[
            pl.BlockSpec((channels, 2 * channels), lambda j: (j // 2, 0)),
            pl.BlockSpec((2 * channels, count), whole),
        ],
        out_shape=[
            jax.ShapeDtypeStruct(
                (packed_rows, 2 * channels), jnp.bfloat16 if has_plan() else jnp.float32
            ),
            jax.ShapeDtypeStruct((2 * channels, count), jnp.bfloat16),
        ],
        scratch_shapes=[pltpu.VMEM((channels, count), jnp.float32)] * 2,
        compiler_params=pltpu.CompilerParams(vmem_limit_bytes=48 * 1024 * 1024),
    )(before, own, after, wide, ids_out, ids_in, conv_weight)


UNIT = 16
PIECES = (5 * UNIT, 4 * UNIT)
FAR = 4


def reduce_kernel(x_ref, out_ref, acc, got_core, got_one, got_two, got_far, send, recv):
    v, r = lax.axis_index("vox"), lax.axis_index("rep")
    z, x = v // 2, v % 2
    y, core = r // 2, r % 2
    core_peer = (v, y * 2 + (1 - core))
    y_peer = (v, (1 - y) * 2 + core)
    x_peer = (z * 2 + (1 - x), r)
    far_peers = [(((z + k) % FAR) * 2 + x, r) for k in range(1, FAR)]
    mesh_ids = pl.DeviceIdType.MESH

    barrier = pltpu.get_barrier_semaphore()
    peers = [core_peer, y_peer, x_peer] + far_peers
    for peer in peers:
        pl.semaphore_signal(barrier, inc=1, device_id=peer, device_id_type=mesh_ids)
    pl.semaphore_wait(barrier, len(peers))

    used = [0]

    def push(source, target, peer):
        at = used[0]
        used[0] += 1
        copy = pltpu.make_async_remote_copy(
            src_ref=source,
            dst_ref=target,
            send_sem=send.at[at],
            recv_sem=recv.at[at],
            device_id=peer,
            device_id_type=mesh_ids,
        )
        copy.start()
        return copy

    def at(start, size):
        return pl.ds(pl.multiple_of(start, UNIT), size)

    def add(target, target_at, left, left_at, others, size):
        chunk = 80 if size % 80 == 0 else 64

        def body(i, carry):
            step = i * chunk
            total = left[at(left_at + step, chunk), :].astype(jnp.float32)
            for ref, ref_at in others:
                total += ref[at(ref_at + step, chunk), :].astype(jnp.float32)
            target[at(target_at + step, chunk), :] = total.astype(target.dtype)
            return carry

        lax.fori_loop(0, size // chunk, body, 0)

    half = 4 * FAR * sum(PIECES)
    base = [0, 4 * FAR * PIECES[0]]
    whole = [4 * FAR * p for p in PIECES]
    first_peer, second_peer = (y_peer, x_peer), (x_peer, y_peer)
    first_bit, second_bit = (y, x), (x, y)
    mine, other = core * half, (1 - core) * half
    sent = []

    core_copies = [
        push(x_ref.at[at(other + base[s], whole[s])], got_core.at[at(base[s], whole[s])], core_peer)
        for s in (0, 1)
    ]
    ones = []
    for s in (0, 1):
        core_copies[s].wait_recv()
        size = whole[s] // 2
        away = base[s] + (1 - first_bit[s]) * size
        add(acc, away, x_ref, mine + away, [(got_core, away)], size)
        ones.append(
            push(
                acc.at[at(away, size)],
                got_one.at[at(base[s] // 2, size)],
                first_peer[s],
            )
        )
        stay = base[s] + first_bit[s] * size
        add(acc, stay, x_ref, mine + stay, [(got_core, stay)], size)
    twos = []
    for s in (0, 1):
        ones[s].wait_recv()
        size = whole[s] // 4
        start = base[s] + first_bit[s] * (whole[s] // 2)
        away = (1 - second_bit[s]) * size
        add(acc, start + away, acc, start + away, [(got_one, base[s] // 2 + away)], size)
        twos.append(
            push(
                acc.at[at(start + away, size)],
                got_two.at[at(base[s] // 4, size)],
                second_peer[s],
            )
        )
        stay = second_bit[s] * size
        add(acc, start + stay, acc, start + stay, [(got_one, base[s] // 2 + stay)], size)
    fars = []
    for s in (0, 1):
        twos[s].wait_recv()
        size = whole[s] // 4
        start = base[s] + first_bit[s] * (whole[s] // 2) + second_bit[s] * size
        add(acc, start, acc, start, [(got_two, base[s] // 4)], size)
        copies = []
        for k in range(1, FAR):
            theirs = (z + k) % FAR
            copies.append(
                push(
                    acc.at[at(start + theirs * PIECES[s], PIECES[s])],
                    got_far.at[at((k - 1) * sum(PIECES) + s * PIECES[0], PIECES[s])],
                    far_peers[k - 1],
                )
            )
        fars.append(copies)
    back = []
    for s in (0, 1):
        for copy in fars[s]:
            copy.wait_recv()
        start = base[s] + first_bit[s] * (whole[s] // 2) + second_bit[s] * (whole[s] // 4)
        piece = start + z * PIECES[s]
        add(
            out_ref,
            mine + piece,
            acc,
            piece,
            [(got_far, k * sum(PIECES) + s * PIECES[0]) for k in range(FAR - 1)],
            PIECES[s],
        )
        span = at(mine + piece, PIECES[s])
        back.append([push(out_ref.at[span], out_ref.at[span], peer) for peer in far_peers])
    two_back = []
    for s in (0, 1):
        for copy in back[s]:
            copy.wait_recv()
        size = whole[s] // 4
        start = base[s] + first_bit[s] * (whole[s] // 2) + second_bit[s] * size
        span = at(mine + start, size)
        two_back.append(push(out_ref.at[span], out_ref.at[span], second_peer[s]))
    one_back = []
    for s in (0, 1):
        two_back[s].wait_recv()
        size = whole[s] // 2
        span = at(mine + base[s] + first_bit[s] * size, size)
        one_back.append(push(out_ref.at[span], out_ref.at[span], first_peer[s]))
    core_back = []
    for s in (0, 1):
        one_back[s].wait_recv()
        span = at(mine + base[s], whole[s])
        core_back.append(push(out_ref.at[span], out_ref.at[span], core_peer))
    for copy in core_back:
        copy.wait_recv()
    for copy in core_copies + ones + twos + fars[0] + fars[1]:
        copy.wait_send()
    for copy in back[0] + back[1] + two_back + one_back + core_back:
        copy.wait_send()


def reduce_call(partial):
    rows, columns = partial.shape
    assert rows == 8 * FAR * sum(PIECES)
    copies = 6 + 2 * (FAR - 1) + 6 + 2 * (FAR - 1)
    kind = partial.dtype
    return pl.pallas_call(
        reduce_kernel,
        in_specs=[pl.BlockSpec(memory_space=pltpu.VMEM)],
        out_specs=pl.BlockSpec(memory_space=pltpu.VMEM),
        out_shape=jax.ShapeDtypeStruct(partial.shape, kind),
        scratch_shapes=[
            pltpu.VMEM((rows // 2, columns), kind),
            pltpu.VMEM((rows // 2, columns), kind),
            pltpu.VMEM((rows // 4, columns), kind),
            pltpu.VMEM((rows // 8, columns), kind),
            pltpu.VMEM(((FAR - 1) * sum(PIECES), columns), kind),
            pltpu.SemaphoreType.DMA((copies,)),
            pltpu.SemaphoreType.DMA((copies,)),
        ],
        compiler_params=pltpu.CompilerParams(
            collective_id=0, has_side_effects=True, vmem_limit_bytes=40 * 1024 * 1024
        ),
    )(partial)


def group_kernel(fine, cot, occupied, down_w, up_w, grouped, cot_groups, values, *wide):
    kids, count, channels = grouped.shape
    cuts = [(c, min(c + 128, channels)) for c in range(0, channels, 128)]
    wide_fine, wide_cot = wide[: len(cuts)], wide[len(cuts) :]
    for source, parts in ((fine, wide_fine), (cot, wide_cot)):
        for part, (low, high) in zip(parts, cuts):
            part[:, : high - low] = source[:, low:high].astype(jnp.float32)

    def child(parts, k):
        pieces = [
            part[pl.ds(k, count, stride=kids), :][:, : high - low]
            for part, (low, high) in zip(parts, cuts)
        ]
        return jnp.concatenate(pieces, 1)

    pre = jnp.zeros((count, channels), jnp.float32)
    back = jnp.zeros((count, channels), jnp.float32)
    for k in range(kids):
        mask = occupied[:, k : k + 1]
        rows = (child(wide_fine, k) * mask).astype(jnp.bfloat16)
        grouped[k] = rows
        pre += dot(rows, down_w[k], ((1,), (0,)))
        rows = (child(wide_cot, k) * mask).astype(jnp.bfloat16)
        cot_groups[k] = rows
        back += dot(rows, up_w[k], ((1,), (1,)))
    values[:, :channels] = pre
    values[:, channels:] = back


def group_call(fine, cot, occupied, down_w, up_w):
    kids, channels = down_w.shape[:2]
    count = occupied.shape[0]
    return pl.pallas_call(
        group_kernel,
        in_specs=[pl.BlockSpec(memory_space=pltpu.VMEM)] * 5,
        out_specs=[pl.BlockSpec(memory_space=pltpu.VMEM)] * 3,
        out_shape=[
            jax.ShapeDtypeStruct((kids, count, channels), jnp.bfloat16),
            jax.ShapeDtypeStruct((kids, count, channels), jnp.bfloat16),
            jax.ShapeDtypeStruct((count, 2 * channels), jnp.float32),
        ],
        scratch_shapes=[pltpu.VMEM((fine.shape[0], 128), jnp.float32)]
        * (2 * (-(-channels // 128))),
        compiler_params=pltpu.CompilerParams(vmem_limit_bytes=40 * 1024 * 1024),
    )(fine, cot, occupied, down_w, up_w)


def outer_kernel(kids, up_rows, down_rows, cot_groups, grouped, packed, out):
    del packed
    channels = up_rows.shape[0]
    step = pl.program_id(0)

    @pl.when(step < kids)
    def _():
        out[:, :channels] = dot(up_rows[...], cot_groups[0], ((1,), (0,))).astype(out.dtype)
        out[:, channels:] = dot(grouped[0], down_rows[...], ((0,), (0,))).astype(out.dtype)

    @pl.when(step >= kids)
    def _():
        out[...] = jnp.zeros_like(out)


def outer_call(taken, up_rows, down_rows, cot_groups, grouped, packed):
    kids, count, channels = grouped.shape
    blocks = packed.shape[0] // channels
    kid = lambda p: (jnp.minimum(p, kids - 1), 0, 0)
    return pl.pallas_call(
        functools.partial(outer_kernel, kids),
        grid=(blocks - taken,),
        in_specs=[
            pl.BlockSpec((channels, count), lambda p: (0, 0)),
            pl.BlockSpec((count, channels), lambda p: (0, 0)),
            pl.BlockSpec((1, count, channels), kid),
            pl.BlockSpec((1, count, channels), kid),
            pl.BlockSpec(memory_space=pl.ANY),
        ],
        out_specs=pl.BlockSpec((channels, 2 * channels), lambda p: (taken + p, 0)),
        out_shape=jax.ShapeDtypeStruct(packed.shape, packed.dtype),
        input_output_aliases={4: 0},
    )(up_rows, down_rows, cot_groups, grouped, packed)


def has_plan():
    return lax.axis_size("vox") == 2 * FAR and lax.axis_size("rep") == 4


def total_gradients(packed):
    if has_plan():
        return reduce_call(packed)
    return lax.psum(packed, ("vox", "rep")).astype(jnp.bfloat16)


def per_device(
    fine_feats, occupancy, parent, neighbors, cotangent, down_weight, conv_weight, up_weight
):
    fine_rows = fine_feats[0]
    occupied = occupancy[0]
    parents = parent[0]
    near_ids = neighbors[0]
    cot_rows = cotangent[0]
    channels = fine_rows.shape[1]
    count = parents.shape[0]
    vox_count = lax.axis_size("vox")
    slots = vox_count * CAP
    own_index = lax.axis_index("vox")
    up = [(i, i + 1) for i in range(vox_count - 1)]
    down = [(j, i) for i, j in up]
    exact = lax.Precision.HIGHEST

    near_next = near_ids + 1
    lists = jnp.concatenate(
        [lax.ppermute(near_next, "vox", up), near_next, lax.ppermute(near_next, "vox", down)], 1
    )
    ids_in = (lists - 1 - own_index * count)[:, None, :]
    ids_out = jnp.where(near_ids < 0, -1, near_ids - (own_index - 1) * count)[:, None, :]

    owner = parents // count
    local_id = parents % count
    remote = owner != own_index
    owner_hits = (
        (owner[:, None] == jnp.arange(vox_count, dtype=jnp.int32)[None, :]) & remote[:, None]
    ).astype(jnp.int32)
    ranks = jnp.cumsum(owner_hits, axis=0) - 1
    slot = jnp.sum(ranks * owner_hits, axis=1)
    dest = jnp.where(remote, owner * CAP + slot, slots)
    place = jnp.arange(slots, dtype=jnp.int32)[:, None] == dest[None, :]
    send_ids = jnp.sum(jnp.where(place, local_id[None, :] + 1, 0), axis=1)

    kids = down_weight.shape[0]
    up_first = jnp.transpose(up_weight, (1, 0, 2))
    grouped, cot_groups, values = group_call(
        fine_rows,
        cot_rows,
        occupied.reshape(count, kids).astype(jnp.float32),
        down_weight,
        up_first,
    )
    send = dot(place.astype(jnp.float32), values, ((1,), (0,)), exact)
    tail = jnp.broadcast_to(send_ids.astype(jnp.float32)[:, None], (slots, 128))
    send = jnp.concatenate([send, tail], 1).reshape(vox_count, CAP, 2 * channels + 128)
    got = lax.all_to_all(send, "vox", split_axis=0, concat_axis=0, tiled=True)
    got = got.reshape(slots, 2 * channels + 128)
    recv_index = got[:, 2 * channels].astype(jnp.int32) - 1
    coarse_ids = jnp.arange(count, dtype=jnp.int32)[:, None]
    keep = coarse_ids == jnp.where(remote, -1, local_id)[None, :]
    arrived = coarse_ids == recv_index[None, :]
    wide = dot(values, keep.astype(jnp.float32), ((0,), (1,)), exact) + dot(
        got[:, : 2 * channels], arrived.astype(jnp.float32), ((0,), (1,)), exact
    )
    own = jnp.concatenate([jax.nn.silu(wide[:channels]), wide[channels:]], 0).astype(jnp.bfloat16)
    before = lax.ppermute(own, "vox", up)
    after = lax.ppermute(own, "vox", down)
    offsets = conv_weight.shape[0]
    taken = (offsets + 1) // 2
    packed_rows = 8 * FAR * sum(PIECES)
    packed, both = conv_call(packed_rows, before, own, after, wide, ids_out, ids_in, conv_weight)

    outgoing = dot(arrived.astype(jnp.bfloat16), both, ((0,), (1,))).astype(jnp.bfloat16)
    returned = lax.all_to_all(
        outgoing.reshape(vox_count, CAP, 2 * channels),
        "vox",
        split_axis=0,
        concat_axis=0,
        tiled=True,
    ).reshape(slots, 2 * channels)
    keep_half, place_half = keep.astype(jnp.bfloat16), place.astype(jnp.bfloat16)
    up_rows = dot(both[:channels], keep_half, ((1,), (0,))) + dot(
        returned[:, :channels], place_half, ((0,), (0,))
    )
    down_rows = dot(keep_half, both[channels:], ((0,), (1,))) + dot(
        place_half, returned[:, channels:], ((0,), (0,))
    )
    packed = outer_call(
        taken,
        up_rows.astype(jnp.bfloat16),
        down_rows.astype(jnp.bfloat16),
        cot_groups,
        grouped,
        packed,
    )
    done = total_gradients(packed)
    pairs = done[: taken * channels].reshape(taken, channels, 2 * channels)
    conv_total = jnp.stack([pairs[:, :, :channels], pairs[:, :, channels:]], 1)
    conv_total = conv_total.reshape(-1, channels, channels)
    rest = done[taken * channels : (taken + kids) * channels]
    up_total = rest[:, :channels].reshape(kids, channels, channels)
    return (
        rest[:, channels:].reshape(kids, channels, channels),
        conv_total[:offsets],
        jnp.transpose(up_total, (1, 0, 2)),
    )


def solution(mesh):
    return jax.shard_map(
        per_device,
        mesh=mesh,
        in_specs=(
            P("rep", "vox", None),
            P("rep", "vox"),
            P("rep", "vox"),
            P("rep", None, "vox"),
            P("rep", "vox", None),
            P(),
            P(),
            P(),
        ),
        out_specs=(P(), P(), P()),
        check_vma=False,
    )
```

```python
import functools

import jax
import jax.numpy as jnp
from jax import lax
from jax.experimental import pallas as pl
from jax.experimental.pallas import tpu as pltpu
from jax.sharding import PartitionSpec as P

CAP = 2


def dot(left, right, dims, precision=None):
    return lax.dot_general(
        left, right, (dims, ((), ())), precision=precision, preferred_element_type=jnp.float32
    )


def conv_kernel(
    before, own, after, wide, ids_out, ids_in, weight, term_ref, both_ref, acc_up, acc_down
):
    step = pl.program_id(0)
    channels, count = acc_up.shape

    @pl.when(step == 0)
    def _():
        acc_up[...] = jnp.zeros_like(acc_up)
        acc_down[...] = jnp.zeros_like(acc_down)

    rows = lax.broadcasted_iota(jnp.int32, (count, count), 0).astype(jnp.int16)

    def hot(ids):
        near = jnp.clip(ids, -1, count).astype(jnp.int16)
        return jnp.where(rows == near, jnp.bfloat16(1), jnp.bfloat16(0))

    weight_here = weight[0]
    gathered = jnp.zeros((channels, count), jnp.float32)
    spread = acc_down[...]
    for at, block in enumerate((before, own, after)):
        gathered += dot(
            block[:channels, :], hot(ids_out[0] - at * count), ((1,), (0,))
        )
        moved = dot(weight_here, block[channels:, :], ((1,), (0,))).astype(jnp.bfloat16)
        spread += dot(moved, hot(ids_in[0, :, at * count : (at + 1) * count]), ((1,), (1,)))
    acc_down[...] = spread
    gathered = gathered.astype(jnp.bfloat16)
    acc_up[...] += dot(weight_here, gathered, ((0,), (0,)))
    term = dot(gathered, own[channels:, :], ((1,), (1,))).astype(term_ref.dtype)

    @pl.when(step % 2 == 0)
    def _():
        term_ref[:, :channels] = term
        term_ref[:, channels:] = jnp.zeros_like(term)

    @pl.when(step % 2 == 1)
    def _():
        term_ref[:, channels:] = term

    @pl.when(step == pl.num_programs(0) - 1)
    def _():
        upper = own[:channels, :].astype(jnp.float32) + acc_up[...]
        both_ref[:channels, :] = upper.astype(jnp.bfloat16)
        pre = wide[:channels, :]
        sig = jax.nn.sigmoid(pre)
        slope = sig * (1.0 + pre * (1.0 - sig))
        both_ref[channels:, :] = ((wide[channels:, :] + acc_down[...]) * slope).astype(
            jnp.bfloat16
        )


def conv_call(packed_rows, before, own, after, wide, ids_out, ids_in, conv_weight):
    offsets, channels = conv_weight.shape[:2]
    count = own.shape[1]
    whole = lambda j: (0, 0)
    each = lambda j: (j, 0, 0)
    return pl.pallas_call(
        conv_kernel,
        grid=(offsets,),
        in_specs=[pl.BlockSpec((2 * channels, count), whole)] * 4
        + [
            pl.BlockSpec((1, 1, count), each),
            pl.BlockSpec((1, 1, 3 * count), each),
            pl.BlockSpec((1, channels, channels), each),
        ],
        out_specs=[
            pl.BlockSpec((channels, 2 * channels), lambda j: (j // 2, 0)),
            pl.BlockSpec((2 * channels, count), whole),
        ],
        out_shape=[
            jax.ShapeDtypeStruct(
                (packed_rows, 2 * channels), jnp.bfloat16 if has_plan() else jnp.float32
            ),
            jax.ShapeDtypeStruct((2 * channels, count), jnp.bfloat16),
        ],
        scratch_shapes=[pltpu.VMEM((channels, count), jnp.float32)] * 2,
        compiler_params=pltpu.CompilerParams(vmem_limit_bytes=48 * 1024 * 1024),
    )(before, own, after, wide, ids_out, ids_in, conv_weight)


UNIT = 16
PIECES = (3 * UNIT, 2 * UNIT, 2 * UNIT, 2 * UNIT)
STREAMS = range(len(PIECES))
FAR = 4


def reduce_kernel(x_ref, out_ref, acc, got_core, got_one, got_two, got_far, send, recv):
    v, r = lax.axis_index("vox"), lax.axis_index("rep")
    z, x = v // 2, v % 2
    y, core = r // 2, r % 2
    core_peer = (v, y * 2 + (1 - core))
    y_peer = (v, (1 - y) * 2 + core)
    x_peer = (z * 2 + (1 - x), r)
    far_peers = [(((z + k) % FAR) * 2 + x, r) for k in range(1, FAR)]
    mesh_ids = pl.DeviceIdType.MESH

    barrier = pltpu.get_barrier_semaphore()
    peers = [core_peer, y_peer, x_peer] + far_peers
    for peer in peers:
        pl.semaphore_signal(barrier, inc=1, device_id=peer, device_id_type=mesh_ids)
    pl.semaphore_wait(barrier, len(peers))

    used = [0]

    def push(source, target, peer):
        at = used[0]
        used[0] += 1
        copy = pltpu.make_async_remote_copy(
            src_ref=source,
            dst_ref=target,
            send_sem=send.at[at],
            recv_sem=recv.at[at],
            device_id=peer,
            device_id_type=mesh_ids,
        )
        copy.start()
        return copy

    def at(start, size):
        return pl.ds(pl.multiple_of(start, UNIT), size)

    def add(target, target_at, left, left_at, others, size):
        chunk = 48 if size % 48 == 0 else 32

        def body(i, carry):
            step = i * chunk
            total = left[at(left_at + step, chunk), :].astype(jnp.float32)
            for ref, ref_at in others:
                total += ref[at(ref_at + step, chunk), :].astype(jnp.float32)
            target[at(target_at + step, chunk), :] = total.astype(target.dtype)
            return carry

        lax.fori_loop(0, size // chunk, body, 0)

    half = 4 * FAR * sum(PIECES)
    base = [4 * FAR * sum(PIECES[:s]) for s in STREAMS]
    whole = [4 * FAR * p for p in PIECES]
    first_peer, second_peer = (y_peer, x_peer) * 2, (x_peer, y_peer) * 2
    first_bit, second_bit = (y, x) * 2, (x, y) * 2
    mine, other = core * half, (1 - core) * half
    sent = []

    core_copies = [
        push(x_ref.at[at(other + base[s], whole[s])], got_core.at[at(base[s], whole[s])], core_peer)
        for s in STREAMS
    ]
    ones = []
    for s in STREAMS:
        core_copies[s].wait_recv()
        size = whole[s] // 2
        away = base[s] + (1 - first_bit[s]) * size
        add(acc, away, x_ref, mine + away, [(got_core, away)], size)
        ones.append(
            push(
                acc.at[at(away, size)],
                got_one.at[at(base[s] // 2, size)],
                first_peer[s],
            )
        )
        stay = base[s] + first_bit[s] * size
        add(acc, stay, x_ref, mine + stay, [(got_core, stay)], size)
    twos = []
    for s in STREAMS:
        ones[s].wait_recv()
        size = whole[s] // 4
        start = base[s] + first_bit[s] * (whole[s] // 2)
        away = (1 - second_bit[s]) * size
        add(acc, start + away, acc, start + away, [(got_one, base[s] // 2 + away)], size)
        twos.append(
            push(
                acc.at[at(start + away, size)],
                got_two.at[at(base[s] // 4, size)],
                second_peer[s],
            )
        )
        stay = second_bit[s] * size
        add(acc, start + stay, acc, start + stay, [(got_one, base[s] // 2 + stay)], size)
    fars = []
    for s in STREAMS:
        twos[s].wait_recv()
        size = whole[s] // 4
        start = base[s] + first_bit[s] * (whole[s] // 2) + second_bit[s] * size
        add(acc, start, acc, start, [(got_two, base[s] // 4)], size)
        copies = []
        for k in range(1, FAR):
            theirs = (z + k) % FAR
            copies.append(
                push(
                    acc.at[at(start + theirs * PIECES[s], PIECES[s])],
                    got_far.at[at((k - 1) * sum(PIECES) + sum(PIECES[:s]), PIECES[s])],
                    far_peers[k - 1],
                )
            )
        fars.append(copies)
    back = []
    for s in STREAMS:
        for copy in fars[s]:
            copy.wait_recv()
        start = base[s] + first_bit[s] * (whole[s] // 2) + second_bit[s] * (whole[s] // 4)
        piece = start + z * PIECES[s]
        add(
            out_ref,
            mine + piece,
            acc,
            piece,
            [(got_far, k * sum(PIECES) + sum(PIECES[:s])) for k in range(FAR - 1)],
            PIECES[s],
        )
        span = at(mine + piece, PIECES[s])
        back.append([push(out_ref.at[span], out_ref.at[span], peer) for peer in far_peers])
    two_back = []
    for s in STREAMS:
        for copy in back[s]:
            copy.wait_recv()
        size = whole[s] // 4
        start = base[s] + first_bit[s] * (whole[s] // 2) + second_bit[s] * size
        span = at(mine + start, size)
        two_back.append(push(out_ref.at[span], out_ref.at[span], second_peer[s]))
    one_back = []
    for s in STREAMS:
        two_back[s].wait_recv()
        size = whole[s] // 2
        span = at(mine + base[s] + first_bit[s] * size, size)
        one_back.append(push(out_ref.at[span], out_ref.at[span], first_peer[s]))
    core_back = []
    for s in STREAMS:
        one_back[s].wait_recv()
        span = at(mine + base[s], whole[s])
        core_back.append(push(out_ref.at[span], out_ref.at[span], core_peer))
    for copy in core_back:
        copy.wait_recv()
    for copy in core_copies + ones + twos + sum(fars + back, []):
        copy.wait_send()
    for copy in two_back + one_back + core_back:
        copy.wait_send()


def reduce_call(partial):
    rows, columns = partial.shape
    assert rows == 8 * FAR * sum(PIECES)
    copies = len(PIECES) * 2 * (3 + FAR - 1)
    kind = partial.dtype
    return pl.pallas_call(
        reduce_kernel,
        in_specs=[pl.BlockSpec(memory_space=pltpu.VMEM)],
        out_specs=pl.BlockSpec(memory_space=pltpu.VMEM),
        out_shape=jax.ShapeDtypeStruct(partial.shape, kind),
        scratch_shapes=[
            pltpu.VMEM((rows // 2, columns), kind),
            pltpu.VMEM((rows // 2, columns), kind),
            pltpu.VMEM((rows // 4, columns), kind),
            pltpu.VMEM((rows // 8, columns), kind),
            pltpu.VMEM(((FAR - 1) * sum(PIECES), columns), kind),
            pltpu.SemaphoreType.DMA((copies,)),
            pltpu.SemaphoreType.DMA((copies,)),
        ],
        compiler_params=pltpu.CompilerParams(
            collective_id=0, has_side_effects=True, vmem_limit_bytes=40 * 1024 * 1024
        ),
    )(partial)


def group_kernel(fine, cot, occupied, down_w, up_w, grouped, cot_groups, values, *wide):
    kids, count, channels = grouped.shape
    cuts = [(c, min(c + 128, channels)) for c in range(0, channels, 128)]
    wide_fine, wide_cot = wide[: len(cuts)], wide[len(cuts) :]
    for source, parts in ((fine, wide_fine), (cot, wide_cot)):
        for part, (low, high) in zip(parts, cuts):
            part[:, : high - low] = source[:, low:high].astype(jnp.float32)

    def child(parts, k):
        pieces = [
            part[pl.ds(k, count, stride=kids), :][:, : high - low]
            for part, (low, high) in zip(parts, cuts)
        ]
        return jnp.concatenate(pieces, 1)

    pre = jnp.zeros((count, channels), jnp.float32)
    back = jnp.zeros((count, channels), jnp.float32)
    for k in range(kids):
        mask = occupied[:, k : k + 1]
        rows = (child(wide_fine, k) * mask).astype(jnp.bfloat16)
        grouped[k] = rows
        pre += dot(rows, down_w[k], ((1,), (0,)))
        rows = (child(wide_cot, k) * mask).astype(jnp.bfloat16)
        cot_groups[k] = rows
        back += dot(rows, up_w[k], ((1,), (1,)))
    values[:, :channels] = pre
    values[:, channels:] = back


def group_call(fine, cot, occupied, down_w, up_w):
    kids, channels = down_w.shape[:2]
    count = occupied.shape[0]
    return pl.pallas_call(
        group_kernel,
        in_specs=[pl.BlockSpec(memory_space=pltpu.VMEM)] * 5,
        out_specs=[pl.BlockSpec(memory_space=pltpu.VMEM)] * 3,
        out_shape=[
            jax.ShapeDtypeStruct((kids, count, channels), jnp.bfloat16),
            jax.ShapeDtypeStruct((kids, count, channels), jnp.bfloat16),
            jax.ShapeDtypeStruct((count, 2 * channels), jnp.float32),
        ],
        scratch_shapes=[pltpu.VMEM((fine.shape[0], 128), jnp.float32)]
        * (2 * (-(-channels // 128))),
        compiler_params=pltpu.CompilerParams(vmem_limit_bytes=40 * 1024 * 1024),
    )(fine, cot, occupied, down_w, up_w)


def outer_kernel(kids, up_rows, down_rows, cot_groups, grouped, packed, out):
    del packed
    channels = up_rows.shape[0]
    step = pl.program_id(0)

    @pl.when(step < kids)
    def _():
        out[:, :channels] = dot(up_rows[...], cot_groups[0], ((1,), (0,))).astype(out.dtype)
        out[:, channels:] = dot(grouped[0], down_rows[...], ((0,), (0,))).astype(out.dtype)

    @pl.when(step >= kids)
    def _():
        out[...] = jnp.zeros_like(out)


def outer_call(taken, up_rows, down_rows, cot_groups, grouped, packed):
    kids, count, channels = grouped.shape
    blocks = packed.shape[0] // channels
    kid = lambda p: (jnp.minimum(p, kids - 1), 0, 0)
    return pl.pallas_call(
        functools.partial(outer_kernel, kids),
        grid=(blocks - taken,),
        in_specs=[
            pl.BlockSpec((channels, count), lambda p: (0, 0)),
            pl.BlockSpec((count, channels), lambda p: (0, 0)),
            pl.BlockSpec((1, count, channels), kid),
            pl.BlockSpec((1, count, channels), kid),
            pl.BlockSpec(memory_space=pl.ANY),
        ],
        out_specs=pl.BlockSpec((channels, 2 * channels), lambda p: (taken + p, 0)),
        out_shape=jax.ShapeDtypeStruct(packed.shape, packed.dtype),
        input_output_aliases={4: 0},
    )(up_rows, down_rows, cot_groups, grouped, packed)


def has_plan():
    return lax.axis_size("vox") == 2 * FAR and lax.axis_size("rep") == 4


def total_gradients(packed):
    if has_plan():
        return reduce_call(packed)
    return lax.psum(packed, ("vox", "rep")).astype(jnp.bfloat16)


def per_device(
    fine_feats, occupancy, parent, neighbors, cotangent, down_weight, conv_weight, up_weight
):
    fine_rows = fine_feats[0]
    occupied = occupancy[0]
    parents = parent[0]
    near_ids = neighbors[0]
    cot_rows = cotangent[0]
    channels = fine_rows.shape[1]
    count = parents.shape[0]
    vox_count = lax.axis_size("vox")
    slots = vox_count * CAP
    own_index = lax.axis_index("vox")
    up = [(i, i + 1) for i in range(vox_count - 1)]
    down = [(j, i) for i, j in up]
    exact = lax.Precision.HIGHEST

    near_next = near_ids + 1
    lists = jnp.concatenate(
        [lax.ppermute(near_next, "vox", up), near_next, lax.ppermute(near_next, "vox", down)], 1
    )
    ids_in = (lists - 1 - own_index * count)[:, None, :]
    ids_out = jnp.where(near_ids < 0, -1, near_ids - (own_index - 1) * count)[:, None, :]

    owner = parents // count
    local_id = parents % count
    remote = owner != own_index
    owner_hits = (
        (owner[:, None] == jnp.arange(vox_count, dtype=jnp.int32)[None, :]) & remote[:, None]
    ).astype(jnp.int32)
    ranks = jnp.cumsum(owner_hits, axis=0) - 1
    slot = jnp.sum(ranks * owner_hits, axis=1)
    dest = jnp.where(remote, owner * CAP + slot, slots)
    place = jnp.arange(slots, dtype=jnp.int32)[:, None] == dest[None, :]
    send_ids = jnp.sum(jnp.where(place, local_id[None, :] + 1, 0), axis=1)

    kids = down_weight.shape[0]
    up_first = jnp.transpose(up_weight, (1, 0, 2))
    grouped, cot_groups, values = group_call(
        fine_rows,
        cot_rows,
        occupied.reshape(count, kids).astype(jnp.float32),
        down_weight,
        up_first,
    )
    send = dot(place.astype(jnp.float32), values, ((1,), (0,)), exact)
    tail = jnp.broadcast_to(send_ids.astype(jnp.float32)[:, None], (slots, 128))
    send = jnp.concatenate([send, tail], 1).reshape(vox_count, CAP, 2 * channels + 128)
    got = lax.all_to_all(send, "vox", split_axis=0, concat_axis=0, tiled=True)
    got = got.reshape(slots, 2 * channels + 128)
    recv_index = got[:, 2 * channels].astype(jnp.int32) - 1
    coarse_ids = jnp.arange(count, dtype=jnp.int32)[:, None]
    keep = coarse_ids == jnp.where(remote, -1, local_id)[None, :]
    arrived = coarse_ids == recv_index[None, :]
    wide = dot(values, keep.astype(jnp.float32), ((0,), (1,)), exact) + dot(
        got[:, : 2 * channels], arrived.astype(jnp.float32), ((0,), (1,)), exact
    )
    own = jnp.concatenate([jax.nn.silu(wide[:channels]), wide[channels:]], 0).astype(jnp.bfloat16)
    before = lax.ppermute(own, "vox", up)
    after = lax.ppermute(own, "vox", down)
    offsets = conv_weight.shape[0]
    taken = (offsets + 1) // 2
    packed_rows = 8 * FAR * sum(PIECES)
    packed, both = conv_call(packed_rows, before, own, after, wide, ids_out, ids_in, conv_weight)

    outgoing = dot(arrived.astype(jnp.bfloat16), both, ((0,), (1,))).astype(jnp.bfloat16)
    returned = lax.all_to_all(
        outgoing.reshape(vox_count, CAP, 2 * channels),
        "vox",
        split_axis=0,
        concat_axis=0,
        tiled=True,
    ).reshape(slots, 2 * channels)
    keep_half, place_half = keep.astype(jnp.bfloat16), place.astype(jnp.bfloat16)
    up_rows = dot(both[:channels], keep_half, ((1,), (0,))) + dot(
        returned[:, :channels], place_half, ((0,), (0,))
    )
    down_rows = dot(keep_half, both[channels:], ((0,), (1,))) + dot(
        place_half, returned[:, channels:], ((0,), (0,))
    )
    packed = outer_call(
        taken,
        up_rows.astype(jnp.bfloat16),
        down_rows.astype(jnp.bfloat16),
        cot_groups,
        grouped,
        packed,
    )
    done = total_gradients(packed)
    pairs = done[: taken * channels].reshape(taken, channels, 2 * channels)
    conv_total = jnp.stack([pairs[:, :, :channels], pairs[:, :, channels:]], 1)
    conv_total = conv_total.reshape(-1, channels, channels)
    rest = done[taken * channels : (taken + kids) * channels]
    up_total = rest[:, :channels].reshape(kids, channels, channels)
    return (
        rest[:, channels:].reshape(kids, channels, channels),
        conv_total[:offsets],
        jnp.transpose(up_total, (1, 0, 2)),
    )


def solution(mesh):
    return jax.shard_map(
        per_device,
        mesh=mesh,
        in_specs=(
            P("rep", "vox", None),
            P("rep", "vox"),
            P("rep", "vox"),
            P("rep", None, "vox"),
            P("rep", "vox", None),
            P(),
            P(),
            P(),
        ),
        out_specs=(P(), P(), P()),
        check_vma=False,
    )
```

```python
import functools

import jax
import jax.numpy as jnp
from jax import lax
from jax.experimental import pallas as pl
from jax.experimental.pallas import tpu as pltpu
from jax.sharding import PartitionSpec as P

CAP = 2


def dot(left, right, dims, precision=None):
    return lax.dot_general(
        left, right, (dims, ((), ())), precision=precision, preferred_element_type=jnp.float32
    )


def conv_kernel(
    before, own, after, wide, ids_out, ids_in, weight_even, weight_odd, term_ref, both_ref, acc_up, acc_down
):
    step = pl.program_id(0)
    channels, count = acc_up.shape

    @pl.when(step == 0)
    def _():
        acc_up[...] = jnp.zeros_like(acc_up)
        acc_down[...] = jnp.zeros_like(acc_down)

    rows = lax.broadcasted_iota(jnp.int32, (count, count), 0).astype(jnp.int16)

    def hot(ids):
        near = jnp.clip(ids, -1, count).astype(jnp.int16)
        return jnp.where(rows == near, jnp.bfloat16(1), jnp.bfloat16(0))

    up_part = jnp.zeros((channels, count), jnp.float32)
    spread = acc_down[...]
    for part, weight in enumerate((weight_even, weight_odd)):
        weight_here = weight[0]
        gathered = jnp.zeros((channels, count), jnp.float32)
        for at, block in enumerate((before, own, after)):
            gathered += dot(
                block[:channels, :], hot(ids_out[part] - at * count), ((1,), (0,))
            )
            moved = dot(weight_here, block[channels:, :], ((1,), (0,))).astype(jnp.bfloat16)
            near = ids_in[part, :, at * count : (at + 1) * count]
            spread += dot(moved, hot(near), ((1,), (1,)))
        gathered = gathered.astype(jnp.bfloat16)
        up_part += dot(weight_here, gathered, ((0,), (0,)))
        term = dot(gathered, own[channels:, :], ((1,), (1,)))
        term_ref[:, part * channels : (part + 1) * channels] = term.astype(term_ref.dtype)
    acc_down[...] = spread
    acc_up[...] += up_part

    @pl.when(step == pl.num_programs(0) - 1)
    def _():
        upper = own[:channels, :].astype(jnp.float32) + acc_up[...]
        both_ref[:channels, :] = upper.astype(jnp.bfloat16)
        pre = wide[:channels, :]
        sig = jax.nn.sigmoid(pre)
        slope = sig * (1.0 + pre * (1.0 - sig))
        both_ref[channels:, :] = ((wide[channels:, :] + acc_down[...]) * slope).astype(
            jnp.bfloat16
        )


def conv_call(packed_rows, before, own, after, wide, ids_out, ids_in, conv_weight):
    offsets, channels = conv_weight.shape[:2]
    count = own.shape[1]
    whole = lambda j: (0, 0)
    padded = lambda ids: jnp.pad(ids, ((0, offsets % 2), (0, 0), (0, 0)), constant_values=-1)
    each = lambda j: (j, 0, 0)
    return pl.pallas_call(
        conv_kernel,
        grid=((offsets + 1) // 2,),
        in_specs=[pl.BlockSpec((2 * channels, count), whole)] * 4
        + [
            pl.BlockSpec((2, 1, count), each),
            pl.BlockSpec((2, 1, 3 * count), each),
            pl.BlockSpec((1, channels, channels), lambda j: (2 * j, 0, 0)),
            pl.BlockSpec(
                (1, channels, channels), lambda j: (jnp.minimum(2 * j + 1, offsets - 1), 0, 0)
            ),
        ],
        out_specs=[
            pl.BlockSpec((channels, 2 * channels), lambda j: (j, 0)),
            pl.BlockSpec((2 * channels, count), whole),
        ],
        out_shape=[
            jax.ShapeDtypeStruct(
                (packed_rows, 2 * channels), jnp.bfloat16 if has_plan() else jnp.float32
            ),
            jax.ShapeDtypeStruct((2 * channels, count), jnp.bfloat16),
        ],
        scratch_shapes=[pltpu.VMEM((channels, count), jnp.float32)] * 2,
        compiler_params=pltpu.CompilerParams(vmem_limit_bytes=48 * 1024 * 1024),
    )(before, own, after, wide, padded(ids_out), padded(ids_in), conv_weight, conv_weight)


UNIT = 16
PIECES = (3 * UNIT, 2 * UNIT, 2 * UNIT, 2 * UNIT)
STREAMS = range(len(PIECES))
FAR = 4


def reduce_kernel(x_ref, out_ref, acc, got_core, got_one, got_two, got_far, send, recv):
    v, r = lax.axis_index("vox"), lax.axis_index("rep")
    z, x = v // 2, v % 2
    y, core = r // 2, r % 2
    core_peer = (v, y * 2 + (1 - core))
    y_peer = (v, (1 - y) * 2 + core)
    x_peer = (z * 2 + (1 - x), r)
    far_peers = [(((z + k) % FAR) * 2 + x, r) for k in range(1, FAR)]
    mesh_ids = pl.DeviceIdType.MESH

    barrier = pltpu.get_barrier_semaphore()
    peers = [core_peer, y_peer, x_peer] + far_peers
    for peer in peers:
        pl.semaphore_signal(barrier, inc=1, device_id=peer, device_id_type=mesh_ids)
    pl.semaphore_wait(barrier, len(peers))

    used = [0]

    def push(source, target, peer):
        at = used[0]
        used[0] += 1
        copy = pltpu.make_async_remote_copy(
            src_ref=source,
            dst_ref=target,
            send_sem=send.at[at],
            recv_sem=recv.at[at],
            device_id=peer,
            device_id_type=mesh_ids,
        )
        copy.start()
        return copy

    def at(start, size):
        return pl.ds(pl.multiple_of(start, UNIT), size)

    def add(target, target_at, left, left_at, others, size):
        chunk = 48 if size % 48 == 0 else 32

        def body(i, carry):
            step = i * chunk
            total = left[at(left_at + step, chunk), :].astype(jnp.float32)
            for ref, ref_at in others:
                total += ref[at(ref_at + step, chunk), :].astype(jnp.float32)
            target[at(target_at + step, chunk), :] = total.astype(target.dtype)
            return carry

        lax.fori_loop(0, size // chunk, body, 0)

    half = 4 * FAR * sum(PIECES)
    base = [4 * FAR * sum(PIECES[:s]) for s in STREAMS]
    whole = [4 * FAR * p for p in PIECES]
    first_peer, second_peer = (y_peer, x_peer) * 2, (x_peer, y_peer) * 2
    first_bit, second_bit = (y, x) * 2, (x, y) * 2
    mine, other = core * half, (1 - core) * half
    sent = []

    core_copies = [
        push(x_ref.at[at(other + base[s], whole[s])], got_core.at[at(base[s], whole[s])], core_peer)
        for s in STREAMS
    ]
    ones = []
    for s in STREAMS:
        core_copies[s].wait_recv()
        size = whole[s] // 2
        away = base[s] + (1 - first_bit[s]) * size
        add(acc, away, x_ref, mine + away, [(got_core, away)], size)
        ones.append(
            push(
                acc.at[at(away, size)],
                got_one.at[at(base[s] // 2, size)],
                first_peer[s],
            )
        )
        stay = base[s] + first_bit[s] * size
        add(acc, stay, x_ref, mine + stay, [(got_core, stay)], size)
    twos = []
    for s in STREAMS:
        ones[s].wait_recv()
        size = whole[s] // 4
        start = base[s] + first_bit[s] * (whole[s] // 2)
        away = (1 - second_bit[s]) * size
        add(acc, start + away, acc, start + away, [(got_one, base[s] // 2 + away)], size)
        twos.append(
            push(
                acc.at[at(start + away, size)],
                got_two.at[at(base[s] // 4, size)],
                second_peer[s],
            )
        )
        stay = second_bit[s] * size
        add(acc, start + stay, acc, start + stay, [(got_one, base[s] // 2 + stay)], size)
    fars = []
    for s in STREAMS:
        twos[s].wait_recv()
        size = whole[s] // 4
        start = base[s] + first_bit[s] * (whole[s] // 2) + second_bit[s] * size
        add(acc, start, acc, start, [(got_two, base[s] // 4)], size)
        copies = []
        for k in range(1, FAR):
            theirs = (z + k) % FAR
            copies.append(
                push(
                    acc.at[at(start + theirs * PIECES[s], PIECES[s])],
                    got_far.at[at((k - 1) * sum(PIECES) + sum(PIECES[:s]), PIECES[s])],
                    far_peers[k - 1],
                )
            )
        fars.append(copies)
    back = []
    for s in STREAMS:
        for copy in fars[s]:
            copy.wait_recv()
        start = base[s] + first_bit[s] * (whole[s] // 2) + second_bit[s] * (whole[s] // 4)
        piece = start + z * PIECES[s]
        add(
            out_ref,
            mine + piece,
            acc,
            piece,
            [(got_far, k * sum(PIECES) + sum(PIECES[:s])) for k in range(FAR - 1)],
            PIECES[s],
        )
        span = at(mine + piece, PIECES[s])
        back.append([push(out_ref.at[span], out_ref.at[span], peer) for peer in far_peers])
    two_back = []
    for s in STREAMS:
        for copy in back[s]:
            copy.wait_recv()
        size = whole[s] // 4
        start = base[s] + first_bit[s] * (whole[s] // 2) + second_bit[s] * size
        span = at(mine + start, size)
        two_back.append(push(out_ref.at[span], out_ref.at[span], second_peer[s]))
    one_back = []
    for s in STREAMS:
        two_back[s].wait_recv()
        size = whole[s] // 2
        span = at(mine + base[s] + first_bit[s] * size, size)
        one_back.append(push(out_ref.at[span], out_ref.at[span], first_peer[s]))
    core_back = []
    for s in STREAMS:
        one_back[s].wait_recv()
        span = at(mine + base[s], whole[s])
        core_back.append(push(out_ref.at[span], out_ref.at[span], core_peer))
    for copy in core_back:
        copy.wait_recv()
    for copy in core_copies + ones + twos + sum(fars + back, []):
        copy.wait_send()
    for copy in two_back + one_back + core_back:
        copy.wait_send()


def reduce_call(partial):
    rows, columns = partial.shape
    assert rows == 8 * FAR * sum(PIECES)
    copies = len(PIECES) * 2 * (3 + FAR - 1)
    kind = partial.dtype
    return pl.pallas_call(
        reduce_kernel,
        in_specs=[pl.BlockSpec(memory_space=pltpu.VMEM)],
        out_specs=pl.BlockSpec(memory_space=pltpu.VMEM),
        out_shape=jax.ShapeDtypeStruct(partial.shape, kind),
        scratch_shapes=[
            pltpu.VMEM((rows // 2, columns), kind),
            pltpu.VMEM((rows // 2, columns), kind),
            pltpu.VMEM((rows // 4, columns), kind),
            pltpu.VMEM((rows // 8, columns), kind),
            pltpu.VMEM(((FAR - 1) * sum(PIECES), columns), kind),
            pltpu.SemaphoreType.DMA((copies,)),
            pltpu.SemaphoreType.DMA((copies,)),
        ],
        compiler_params=pltpu.CompilerParams(
            collective_id=0, has_side_effects=True, vmem_limit_bytes=40 * 1024 * 1024
        ),
    )(partial)


def group_kernel(fine, cot, occupied, down_w, up_w, grouped, cot_groups, values, *wide):
    kids, count, channels = grouped.shape
    cuts = [(c, min(c + 128, channels)) for c in range(0, channels, 128)]
    wide_fine, wide_cot = wide[: len(cuts)], wide[len(cuts) :]
    for source, parts in ((fine, wide_fine), (cot, wide_cot)):
        for part, (low, high) in zip(parts, cuts):
            part[:, : high - low] = source[:, low:high].astype(jnp.float32)

    def child(parts, k):
        pieces = [
            part[pl.ds(k, count, stride=kids), :][:, : high - low]
            for part, (low, high) in zip(parts, cuts)
        ]
        return jnp.concatenate(pieces, 1)

    pre = jnp.zeros((count, channels), jnp.float32)
    back = jnp.zeros((count, channels), jnp.float32)
    for k in range(kids):
        mask = occupied[:, k : k + 1]
        rows = (child(wide_fine, k) * mask).astype(jnp.bfloat16)
        grouped[k] = rows
        pre += dot(rows, down_w[k], ((1,), (0,)))
        rows = (child(wide_cot, k) * mask).astype(jnp.bfloat16)
        cot_groups[k] = rows
        back += dot(rows, up_w[k], ((1,), (1,)))
    values[:, :channels] = pre
    values[:, channels:] = back


def group_call(fine, cot, occupied, down_w, up_w):
    kids, channels = down_w.shape[:2]
    count = occupied.shape[0]
    return pl.pallas_call(
        group_kernel,
        in_specs=[pl.BlockSpec(memory_space=pltpu.VMEM)] * 5,
        out_specs=[pl.BlockSpec(memory_space=pltpu.VMEM)] * 3,
        out_shape=[
            jax.ShapeDtypeStruct((kids, count, channels), jnp.bfloat16),
            jax.ShapeDtypeStruct((kids, count, channels), jnp.bfloat16),
            jax.ShapeDtypeStruct((count, 2 * channels), jnp.float32),
        ],
        scratch_shapes=[pltpu.VMEM((fine.shape[0], 128), jnp.float32)]
        * (2 * (-(-channels // 128))),
        compiler_params=pltpu.CompilerParams(vmem_limit_bytes=40 * 1024 * 1024),
    )(fine, cot, occupied, down_w, up_w)


def outer_kernel(kids, up_rows, down_rows, cot_groups, grouped, packed, out):
    del packed
    channels = up_rows.shape[0]
    step = pl.program_id(0)

    @pl.when(step < kids)
    def _():
        out[:, :channels] = dot(up_rows[...], cot_groups[0], ((1,), (0,))).astype(out.dtype)
        out[:, channels:] = dot(grouped[0], down_rows[...], ((0,), (0,))).astype(out.dtype)

    @pl.when(step >= kids)
    def _():
        out[...] = jnp.zeros_like(out)


def outer_call(taken, up_rows, down_rows, cot_groups, grouped, packed):
    kids, count, channels = grouped.shape
    blocks = packed.shape[0] // channels
    kid = lambda p: (jnp.minimum(p, kids - 1), 0, 0)
    return pl.pallas_call(
        functools.partial(outer_kernel, kids),
        grid=(blocks - taken,),
        in_specs=[
            pl.BlockSpec((channels, count), lambda p: (0, 0)),
            pl.BlockSpec((count, channels), lambda p: (0, 0)),
            pl.BlockSpec((1, count, channels), kid),
            pl.BlockSpec((1, count, channels), kid),
            pl.BlockSpec(memory_space=pl.ANY),
        ],
        out_specs=pl.BlockSpec((channels, 2 * channels), lambda p: (taken + p, 0)),
        out_shape=jax.ShapeDtypeStruct(packed.shape, packed.dtype),
        input_output_aliases={4: 0},
    )(up_rows, down_rows, cot_groups, grouped, packed)


def has_plan():
    return lax.axis_size("vox") == 2 * FAR and lax.axis_size("rep") == 4


def total_gradients(packed):
    if has_plan():
        return reduce_call(packed)
    return lax.psum(packed, ("vox", "rep")).astype(jnp.bfloat16)


def per_device(
    fine_feats, occupancy, parent, neighbors, cotangent, down_weight, conv_weight, up_weight
):
    fine_rows = fine_feats[0]
    occupied = occupancy[0]
    parents = parent[0]
    near_ids = neighbors[0]
    cot_rows = cotangent[0]
    channels = fine_rows.shape[1]
    count = parents.shape[0]
    vox_count = lax.axis_size("vox")
    slots = vox_count * CAP
    own_index = lax.axis_index("vox")
    up = [(i, i + 1) for i in range(vox_count - 1)]
    down = [(j, i) for i, j in up]
    exact = lax.Precision.HIGHEST

    near_next = near_ids + 1
    lists = jnp.concatenate(
        [lax.ppermute(near_next, "vox", up), near_next, lax.ppermute(near_next, "vox", down)], 1
    )
    ids_in = (lists - 1 - own_index * count)[:, None, :]
    ids_out = jnp.where(near_ids < 0, -1, near_ids - (own_index - 1) * count)[:, None, :]

    owner = parents // count
    local_id = parents % count
    remote = owner != own_index
    owner_hits = (
        (owner[:, None] == jnp.arange(vox_count, dtype=jnp.int32)[None, :]) & remote[:, None]
    ).astype(jnp.int32)
    ranks = jnp.cumsum(owner_hits, axis=0) - 1
    slot = jnp.sum(ranks * owner_hits, axis=1)
    dest = jnp.where(remote, owner * CAP + slot, slots)
    place = jnp.arange(slots, dtype=jnp.int32)[:, None] == dest[None, :]
    send_ids = jnp.sum(jnp.where(place, local_id[None, :] + 1, 0), axis=1)

    kids = down_weight.shape[0]
    up_first = jnp.transpose(up_weight, (1, 0, 2))
    grouped, cot_groups, values = group_call(
        fine_rows,
        cot_rows,
        occupied.reshape(count, kids).astype(jnp.float32),
        down_weight,
        up_first,
    )
    send = dot(place.astype(jnp.float32), values, ((1,), (0,)), exact)
    tail = jnp.broadcast_to(send_ids.astype(jnp.float32)[:, None], (slots, 128))
    send = jnp.concatenate([send, tail], 1).reshape(vox_count, CAP, 2 * channels + 128)
    got = lax.all_to_all(send, "vox", split_axis=0, concat_axis=0, tiled=True)
    got = got.reshape(slots, 2 * channels + 128)
    recv_index = got[:, 2 * channels].astype(jnp.int32) - 1
    coarse_ids = jnp.arange(count, dtype=jnp.int32)[:, None]
    keep = coarse_ids == jnp.where(remote, -1, local_id)[None, :]
    arrived = coarse_ids == recv_index[None, :]
    wide = dot(values, keep.astype(jnp.float32), ((0,), (1,)), exact) + dot(
        got[:, : 2 * channels], arrived.astype(jnp.float32), ((0,), (1,)), exact
    )
    own = jnp.concatenate([jax.nn.silu(wide[:channels]), wide[channels:]], 0).astype(jnp.bfloat16)
    before = lax.ppermute(own, "vox", up)
    after = lax.ppermute(own, "vox", down)
    offsets = conv_weight.shape[0]
    taken = (offsets + 1) // 2
    packed_rows = 8 * FAR * sum(PIECES)
    packed, both = conv_call(packed_rows, before, own, after, wide, ids_out, ids_in, conv_weight)

    outgoing = dot(arrived.astype(jnp.bfloat16), both, ((0,), (1,))).astype(jnp.bfloat16)
    returned = lax.all_to_all(
        outgoing.reshape(vox_count, CAP, 2 * channels),
        "vox",
        split_axis=0,
        concat_axis=0,
        tiled=True,
    ).reshape(slots, 2 * channels)
    keep_half, place_half = keep.astype(jnp.bfloat16), place.astype(jnp.bfloat16)
    up_rows = dot(both[:channels], keep_half, ((1,), (0,))) + dot(
        returned[:, :channels], place_half, ((0,), (0,))
    )
    down_rows = dot(keep_half, both[channels:], ((0,), (1,))) + dot(
        place_half, returned[:, channels:], ((0,), (0,))
    )
    packed = outer_call(
        taken,
        up_rows.astype(jnp.bfloat16),
        down_rows.astype(jnp.bfloat16),
        cot_groups,
        grouped,
        packed,
    )
    done = total_gradients(packed)
    pairs = done[: taken * channels].reshape(taken, channels, 2 * channels)
    conv_total = jnp.stack([pairs[:, :, :channels], pairs[:, :, channels:]], 1)
    conv_total = conv_total.reshape(-1, channels, channels)
    rest = done[taken * channels : (taken + kids) * channels]
    up_total = rest[:, :channels].reshape(kids, channels, channels)
    return (
        rest[:, channels:].reshape(kids, channels, channels),
        conv_total[:offsets],
        jnp.transpose(up_total, (1, 0, 2)),
    )


def solution(mesh):
    return jax.shard_map(
        per_device,
        mesh=mesh,
        in_specs=(
            P("rep", "vox", None),
            P("rep", "vox"),
            P("rep", "vox"),
            P("rep", None, "vox"),
            P("rep", "vox", None),
            P(),
            P(),
            P(),
        ),
        out_specs=(P(), P(), P()),
        check_vma=False,
    )
```
